256 devices in a mesh: ctx: 32 (over z, x), head: 8 (over y, core).
Axes of the slice: x: 4, y: 4, z: 8, core: 2. Of those that a mesh axis runs over, the one named last changes fastest.
Arguments:
- inputs: bfloat16 [16384, 6144], P('ctx', 'head'), may hold values from -0.046875 to 0.046875
- query: bfloat16 [16384, 8192], P('ctx', 'head'), may hold values from -0.875 to 0.875
- key_rows: bfloat16 [16384, 8192], P('ctx', 'head'), may hold values from -0.875 to 0.875
- value: bfloat16 [16384, 8192], P('ctx', 'head'), may hold values from -0.875 to 0.875
- grad_out: bfloat16 [16384, 8192], P('ctx', 'head'), may hold values from -0.875 to 0.875
- decay_power: int32 [64], replicated, may hold values from 1 to 2048, as said below
Outputs:
- key_grad: float32 [16384, 8192], P('ctx', 'head')
- value_grad: float32 [16384, 8192], P('ctx', 'head')
- query_weight_grad: float32 [6144, 8192], P('ctx', 'head')
The draws below stay inside these ranges and needn't reach their ends.
Inputs may be any that keep to these rules, and one draw needn't show every extreme that they name: `decay_power`: every entry is a power of two.
All inputs are finite; a program needn't handle non-finite values.
Results may differ from the reference program's by a relative error of at most 0.02.
Values may be sent and summed in bfloat16 or wider, within the bound.
A program may use at most 192 MiB of HBM per device.

```python
import math
import jax
import jax.numpy as jnp
from jax import lax

D = 6144
HEADS = 64
HEAD_DIM = 128
BLOCK = 256
TOK_DEV = 512
TOKENS = 16384
INNER = 8192


def draw_decay_power(key, part):
    key = jax.random.fold_in(key, 11)
    first, second, third, fourth = jax.random.split(key, 4)
    slow = jax.random.randint(first, (HEADS,), 0, 4)
    fast = jax.random.randint(second, (HEADS,), 4, 12)
    pick = jax.random.randint(third, (HEADS,), 0, 2)
    level = jnp.where(pick == 0, slow, fast)
    order = jax.random.permutation(fourth, HEADS)
    level = level.at[order[0]].set(0).at[order[1]].set(11)
    return jnp.left_shift(jnp.ones((HEADS,), jnp.int32), level.astype(jnp.int32))


def steps_of(stream_key, shape, cuts, low, top_value):
    level = 1.0
    for axis_at, shards_of in cuts:
        heights = jax.random.uniform(jax.random.fold_in(jax.random.fold_in(stream_key, 6), axis_at), (shards_of,), jnp.float32, low / len(cuts), top_value / len(cuts))
        level = level * jnp.repeat(jnp.exp(heights), shape[axis_at] // shards_of).reshape((-1,) + (1,) * (len(shape) - 1 - axis_at))
    return level


def centred(rng, extent, scale, most, cuts=(), held_as=jnp.bfloat16):
    result = jax.random.normal(rng, extent, jnp.float32) * scale
    if len(cuts) > 0:
        result = steps_of(rng, extent, cuts, -0.22, 0.18) * result
    return jnp.clip(result, min=-most, max=most).astype(held_as)


def setup_inputs(seed: int = 0) -> dict:
    seeds = jax.random.split(jax.random.key(seed), 7)
    return {
        "inputs": centred(seeds[0], (TOKENS, D), TOKENS ** -0.5, 0.046875, ((0, 32), (1, 8))),
        "query": centred(seeds[1], (TOKENS, INNER), 0.15, 0.875, ((0, 32), (1, 8))),
        "key_rows": centred(seeds[2], (TOKENS, INNER), 0.15, 0.875, ((0, 32), (1, 8))),
        "value": centred(seeds[3], (TOKENS, INNER), 0.15, 0.875, ((0, 32), (1, 8))),
        "grad_out": centred(seeds[4], (TOKENS, INNER), 0.15, 0.875, ((0, 32), (1, 8))),
        "decay_power": draw_decay_power(jax.random.fold_in(seeds[6], 71), 0),
    }


HIGH = lax.Precision.HIGHEST


def to_low(array):
    return lax.optimization_barrier(array.astype(jnp.bfloat16)).astype(jnp.float32)


def decayed_sums(query, key_rows, value, grad_out, rates):
    length = query.shape[0]
    place = jnp.arange(length, dtype=jnp.float32)
    tail = jnp.exp(-rates[None, :] * (length - 1.0 - place)[:, None])
    lead = jnp.exp(-rates[None, :] * place[:, None])
    scaled_key = to_low(key_rows.astype(jnp.float32) * tail[:, :, None])
    scaled_query = to_low(query.astype(jnp.float32) * lead[:, :, None])
    memory = jnp.einsum('tha,thc->hac', scaled_key, value.astype(jnp.float32), precision=HIGH)
    backing = jnp.einsum('tha,thc->hac', scaled_query, grad_out.astype(jnp.float32), precision=HIGH)
    return memory, backing


def block_terms(pieces, rates):
    query, key_rows, value, grad_out = pieces
    size = query.shape[0]
    place = jnp.arange(size, dtype=jnp.float32)
    gap = place[:, None] - place[None, :]
    fade = jnp.where(gap[None] >= 0.0, jnp.exp(-rates[:, None, None] * jnp.maximum(gap, 0.0)[None]), 0.0)
    q32 = query.astype(jnp.float32)
    k32 = key_rows.astype(jnp.float32)
    v32 = value.astype(jnp.float32)
    g32 = grad_out.astype(jnp.float32)
    score_a = (jnp.einsum('tha,sha->hts', g32, v32, precision=HIGH) * fade).astype(jnp.bfloat16).astype(jnp.float32)
    score_b = (jnp.einsum('tha,sha->hts', q32, k32, precision=HIGH) * fade).astype(jnp.bfloat16).astype(jnp.float32)
    grad_q = jnp.einsum('hts,sha->tha', score_a, k32, precision=HIGH)
    grad_k = jnp.einsum('hts,tha->sha', score_a, q32, precision=HIGH)
    grad_v = jnp.einsum('hts,tha->sha', score_b, g32, precision=HIGH)
    memory, backing = decayed_sums(query, key_rows, value, grad_out, rates)
    return grad_q, grad_k, grad_v, memory, backing


def span_grads(query, key_rows, value, grad_out, rates, prefix, suffix):
    length, heads, width = query.shape
    count = length // BLOCK
    blocks = tuple(a.reshape(count, BLOCK, heads, width) for a in (query, key_rows, value, grad_out))
    inner_q, inner_k, inner_v, memories, backings = lax.map(lambda pieces: block_terms(pieces, rates), blocks)
    step_fade = jnp.exp(-rates * float(BLOCK))[:, None, None]

    def forward(carry, memory):
        return step_fade * carry + memory, carry

    def backward(carry, backing):
        return step_fade * carry + backing, carry

    unused_a, starts = lax.scan(forward, prefix, memories)
    unused_b, finishes = lax.scan(backward, suffix, backings, reverse=True)
    starts = to_low(starts)
    finishes = to_low(finishes)
    place = jnp.arange(BLOCK, dtype=jnp.float32)
    lead_fade = jnp.exp(-rates[None, :] * (place + 1.0)[:, None])[None, :, :, None]
    back_fade = jnp.exp(-rates[None, :] * (BLOCK - place)[:, None])[None, :, :, None]
    query_b, key_b, value_b, grad_b = blocks
    grad_q = inner_q + lead_fade * jnp.einsum('nhac,nthc->ntha', starts, grad_b.astype(jnp.float32), precision=HIGH)
    grad_k = inner_k + back_fade * jnp.einsum('nhac,nthc->ntha', finishes, value_b.astype(jnp.float32), precision=HIGH)
    grad_v = inner_v + back_fade * jnp.einsum('nhac,ntha->nthc', finishes, key_b.astype(jnp.float32), precision=HIGH)
    shape = (length, heads * width)
    return grad_q.reshape(shape).astype(jnp.bfloat16), grad_k.reshape(shape).astype(jnp.float32), grad_v.reshape(shape).astype(jnp.float32)


def reference(inputs, query, key_rows, value, grad_out, decay_power):
    rates = decay_power.astype(jnp.float32) * (math.log(2.0) / (4.0 * TOKENS))
    spans = TOKENS // TOK_DEV
    shaped = tuple(a.reshape(spans, TOK_DEV, HEADS, HEAD_DIM) for a in (query, key_rows, value, grad_out))

    def states_of(pieces):
        memory, backing = decayed_sums(pieces[0], pieces[1], pieces[2], pieces[3], rates)
        return memory.astype(jnp.bfloat16), backing.astype(jnp.bfloat16)

    memories, backings = lax.map(states_of, shaped)
    memories = memories.astype(jnp.float32)
    backings = backings.astype(jnp.float32)
    order = jnp.arange(spans, dtype=jnp.int32)
    span_rate = rates[None, :] * float(TOK_DEV)

    def sums_for(rank):
        gap_before = jnp.maximum(rank - 1 - order, 0).astype(jnp.float32)
        gap_after = jnp.maximum(order - rank - 1, 0).astype(jnp.float32)
        weight_before = jnp.where((order < rank)[:, None], jnp.exp(-span_rate * gap_before[:, None]), 0.0)
        weight_after = jnp.where((order > rank)[:, None], jnp.exp(-span_rate * gap_after[:, None]), 0.0)
        prefix = jnp.einsum('nh,nhac->hac', weight_before, memories, precision=HIGH)
        suffix = jnp.einsum('nh,nhac->hac', weight_after, backings, precision=HIGH)
        return prefix, suffix

    prefixes, suffixes = lax.map(sums_for, order)
    rows_in = inputs.reshape(spans, TOK_DEV, D)

    def per_span(total, items):
        q_s, k_s, v_s, g_s, x_s, prefix, suffix = items
        grad_q, grad_k, grad_v = span_grads(q_s, k_s, v_s, g_s, rates, prefix, suffix)
        part = jnp.dot(x_s.T, grad_q, preferred_element_type=jnp.float32)
        part = lax.optimization_barrier(part.astype(jnp.bfloat16)).astype(jnp.float32)
        return total + part, (grad_k, grad_v)

    start_total = jnp.zeros((D, INNER), jnp.float32)
    total, outs = lax.scan(per_span, start_total, shaped + (rows_in, prefixes, suffixes))
    key_grad = outs[0].reshape(TOKENS, INNER)
    value_grad = outs[1].reshape(TOKENS, INNER)
    return key_grad, value_grad, total
```

```python
import math

import jax
import jax.numpy as jnp
from jax import lax
from jax.experimental import pallas as pl
from jax.experimental.pallas import tpu as pltpu
from jax.sharding import PartitionSpec as P

X, Z, Y = 4, 8, 4
W = 128
B = 256
T = 2 * B
H = 8
G = 2
HG = H // G
Q = W // X
F = 192
FEATURES = F * Z
MESH = pl.DeviceIdType.MESH
F32, BF16 = jnp.float32, jnp.bfloat16
MEM, BACK = 0, 1


def dot(a, b, ca, cb):
    return lax.dot_general(a, b, (((ca,), (cb,)), ((), ())), preferred_element_type=F32)


def rcopy(src, dst, ss, rs, dev):
    return pltpu.make_async_remote_copy(
        src_ref=src, dst_ref=dst, send_sem=ss, recv_sem=rs, device_id=dev, device_id_type=MESH
    )


def kernel(
    x_hbm, q_hbm, k_hbm, v_hbm, g_hbm, power,
    key_out, value_out, weight_out,
    xin, qv, kv, vv, gv, xown, xt,
    bm0, bb1, memq, s1, lz, gz, out3, p3,
    qi, kg, vg, qg, part, sb, rb, wout,
    ld, xl, xs_s, xs_r, ys_s, ys_r, cs_s, cs_r,
    s1_s, s1_r, s2_s, s2_r, s3_s, s3_r, qg_s, qg_r, rs_s, rs_r, kv_o, w_o,
):
    ctx = lax.axis_index("ctx")
    hd = lax.axis_index("head")
    x, z = lax.rem(ctx, X), ctx // X
    y, core = hd // 2, lax.rem(hd, 2)

    def at_x(d):
        return (z * X + lax.rem(x + d, X), hd)

    def at_z(zt):
        return (zt * X + x, hd)

    def at_y(d):
        return (ctx, lax.rem(y + d, Y) * 2 + core)

    sibling = (ctx, y * 2 + 1 - core)

    loads = [
        pltpu.make_async_copy(src, dst, ld.at[i])
        for i, (src, dst) in enumerate(
            ((k_hbm, kv), (v_hbm, vv), (x_hbm, xin), (q_hbm, qv), (g_hbm, gv))
        )
    ]
    for c in loads:
        c.start()

    barrier = pltpu.get_barrier_semaphore()
    partners = (
        [at_x(d) for d in range(1, X)]
        + [at_z(lax.rem(z + d, Z)) for d in range(1, Z)]
        + [at_y(d) for d in range(1, Y)]
        + [sibling]
    )
    for dev in partners:
        pl.semaphore_signal(barrier, inc=1, device_id=dev, device_id_type=MESH)

    def rate_of(h):
        return power[hd * H + h].astype(F32) * (math.log(2.0) / (4.0 * T * X * Z))

    def decay(rate, count):
        return jnp.exp(jnp.full((1, W), -rate * count, F32))

    def rows():
        return lax.broadcasted_iota(jnp.int32, (B, W), 0).astype(F32)

    def cols(h):
        return pl.ds(pl.multiple_of(h * W, W), W)

    def mem_head(h, carry):
        rate = rate_of(h)
        tail = jnp.exp(-rate * ((B - 1.0) - rows()))
        sums = []
        for b in range(2):
            r = pl.ds(b * B, B)
            low = (kv[r, cols(h)].astype(F32) * tail).astype(BF16)
            sums.append(dot(low, vv[r, cols(h)], 0, 0))
        bm0[h] = sums[0]
        m = (decay(rate, float(B)) * sums[0] + sums[1]).astype(BF16)
        for i in range(X):
            memq[MEM, i, h] = m[i * Q : (i + 1) * Q]
        return carry

    def back_head(h, carry):
        rate = rate_of(h)
        lead = jnp.exp(-rate * rows())
        sums = []
        for b in range(2):
            r = pl.ds(b * B, B)
            low = (qv[r, cols(h)].astype(F32) * lead).astype(BF16)
            sums.append(dot(low, gv[r, cols(h)], 0, 0))
        bb1[h] = sums[1]
        m = (sums[0] + decay(rate, float(B)) * sums[1]).astype(BF16)
        for i in range(X):
            memq[BACK, i, h] = m[i * Q : (i + 1) * Q]
        return carry

    def heads(g):
        return pl.ds(g * HG, HG)

    def stage1(kind, g, d):
        xt_to = lax.rem(x + d, X)
        return rcopy(
            memq.at[kind, xt_to, heads(g)], s1.at[kind, x, heads(g)],
            s1_s.at[kind, g, d - 1], s1_r.at[kind, g, d - 1], at_x(d),
        )

    def stage1_recv(kind, g, d):
        xf = lax.rem(x - d + X, X)
        dst = s1.at[kind, xf, heads(g)]
        rcopy(dst, dst, s1_s.at[kind, g, d - 1], s1_r.at[kind, g, d - 1], at_x(d)).wait_recv()

    def send_stage1(kind):
        s1[kind, x] = memq[kind, x]
        for g in range(G):
            for d in (1, 3, 2):
                stage1(kind, g, d).start()

    def stage2(kind, g, zt):
        return rcopy(
            lz.at[kind, heads(g)], gz.at[z, heads(g)], s2_s.at[g, zt], s2_r.at[g, z], at_z(zt)
        )

    def line_sums(kind, g):
        for d in range(1, X):
            stage1_recv(kind, g, d)

        def one(i, carry):
            h = g * HG + i
            d = decay(rate_of(h), float(T))
            order = range(X) if kind == MEM else range(X - 1, -1, -1)
            total = None
            for xi in order:
                term = s1[kind, xi, h].astype(F32)
                total = term if total is None else total * d + term
            lz[kind, h] = total.astype(BF16)
            return carry

        lax.fori_loop(0, HG, one, 0)

        def send(i, carry):
            zt = z + 1 + i if kind == MEM else z - 1 - i
            stage2(kind, g, zt).start()
            return carry

        lax.fori_loop(0, Z - 1 - z if kind == MEM else z, send, 0)

    def stage3(kind, g, d):
        xt_to = lax.rem(x + d, X)
        return rcopy(
            out3.at[kind, xt_to, heads(g)], p3.at[kind, x, heads(g)],
            s3_s.at[kind, g, d - 1], s3_r.at[kind, g, d - 1], at_x(d),
        )

    def stage3_recv(kind, g, d):
        xf = lax.rem(x - d + X, X)
        dst = p3.at[kind, xf, heads(g)]
        rcopy(dst, dst, s3_s.at[kind, g, d - 1], s3_r.at[kind, g, d - 1], at_x(d)).wait_recv()

    def scans(kind, g):
        count = z if kind == MEM else Z - 1 - z

        def source(i):
            return i if kind == MEM else Z - 1 - i

        def wait(i, carry):
            dst = gz.at[source(i), heads(g)]
            rcopy(dst, dst, s2_s.at[g, 0], s2_r.at[g, source(i)], at_z(source(i))).wait_recv()
            return carry

        lax.fori_loop(0, count, wait, 0)

        def one(i, carry):
            h = g * HG + i
            rate = rate_of(h)
            d, line = decay(rate, float(T)), decay(rate, float(T * X))

            def add(i, total):
                return total * line + gz[source(i), h].astype(F32)

            run = lax.fori_loop(0, count, add, jnp.zeros((Q, W), F32))
            order = range(X) if kind == MEM else range(X - 1, -1, -1)
            for xi in order:
                out3[kind, xi, h] = run.astype(BF16)
                run = run * d + s1[kind, xi, h].astype(F32)
            return carry

        lax.fori_loop(0, HG, one, 0)
        p3[kind, x, heads(g)] = out3[kind, x, heads(g)]
        for d in (1, 3, 2):
            stage3(kind, g, d).start()

    def inner_head(h, carry):
        rate = rate_of(h)
        t = lax.broadcasted_iota(jnp.int32, (B, B), 0)
        s = lax.broadcasted_iota(jnp.int32, (B, B), 1)
        gap = (t - s).astype(F32)
        fade = jnp.where(gap >= 0.0, jnp.exp(-rate * jnp.maximum(gap, 0.0)), 0.0)
        turned = jnp.where(gap <= 0.0, jnp.exp(rate * jnp.minimum(gap, 0.0)), 0.0)
        for b in range(2):
            r = pl.ds(b * B, B)
            qh, kh, vh, gh = (a[r, cols(h)] for a in (qv, kv, vv, gv))
            sa = (dot(gh, vh, 1, 1) * fade).astype(BF16)
            qi[h, r] = dot(sa, kh, 1, 0)
            sat = (dot(vh, gh, 1, 1) * turned).astype(BF16)
            kg[h, r] = dot(sat, qh, 1, 0)
            sbt = (dot(kh, qh, 1, 1) * turned).astype(BF16)
            vg[h, r] = dot(sbt, gh, 1, 0)
        return carry

    def qg_send(h, d):
        mine = qg.at[h, pl.ds(pl.multiple_of(x * T, T), T)]
        return rcopy(mine, mine, qg_s.at[h, d - 1], qg_r.at[h, d - 1], at_x(d))

    def qg_recv(h, d):
        xf = lax.rem(x - d + X, X)
        dst = qg.at[h, pl.ds(pl.multiple_of(xf * T, T), T)]
        rcopy(dst, dst, qg_s.at[h, d - 1], qg_r.at[h, d - 1], at_x(d)).wait_recv()

    def query_head(h, carry):
        rate = rate_of(h)
        lead = jnp.exp(-rate * (rows() + 1.0))
        prefix = p3[MEM, :, h].reshape(W, W)
        starts = (prefix, (decay(rate, float(B)) * prefix.astype(F32) + bm0[h]).astype(BF16))
        for b in range(2):
            r = pl.ds(b * B, B)
            whole = qi[h, r] + lead * dot(gv[r, cols(h)], starts[b], 1, 1)
            qg[h, pl.ds(pl.multiple_of(x * T + b * B, B), B)] = whole.astype(BF16)
        for d in (1, 3, 2):
            qg_send(h, d).start()
        return carry

    def kv_copies(h):
        return (
            pltpu.make_async_copy(kg.at[h], key_out.at[:, cols(h)], kv_o.at[0, h]),
            pltpu.make_async_copy(vg.at[h], value_out.at[:, cols(h)], kv_o.at[1, h]),
        )

    def key_value_head(h, carry):
        rate = rate_of(h)
        fall = jnp.exp(-rate * (float(B) - rows()))
        suffix = p3[BACK, :, h].reshape(W, W)
        finishes = ((decay(rate, float(B)) * suffix.astype(F32) + bb1[h]).astype(BF16), suffix)
        for b in range(2):
            r = pl.ds(b * B, B)
            kg[h, r] += fall * dot(vv[r, cols(h)], finishes[b], 1, 1)
            vg[h, r] += fall * dot(kv[r, cols(h)], finishes[b], 1, 0)
        for c in kv_copies(h):
            c.start()
        return carry

    def x_rows(owner):
        return pl.ds(pl.multiple_of(owner * F, F), F)

    def x_cols(xi):
        return pl.ds(pl.multiple_of(xi * T, T), T)

    def x_send(d):
        return rcopy(
            xown.at[lax.rem(x + d, X)], xt.at[x_rows(hd), x_cols(x)],
            xs_s.at[d - 1], xs_r.at[d - 1], at_x(d),
        )

    def x_recv(d):
        xf = lax.rem(x - d + X, X)
        dst = xt.at[x_rows(hd), x_cols(xf)]
        rcopy(dst, dst, xs_s.at[d - 1], xs_r.at[d - 1], at_x(d)).wait_recv()

    def y_send(xi, d):
        mine = xt.at[x_rows(hd), x_cols(xi)]
        return rcopy(mine, mine, ys_s.at[xi, d - 1], ys_r.at[xi, d - 1], at_y(d))

    def y_recv(xi, d):
        owner = lax.rem(y - d + Y, Y) * 2 + core
        dst = xt.at[x_rows(owner), x_cols(xi)]
        rcopy(dst, dst, ys_s.at[xi, d - 1], ys_r.at[xi, d - 1], at_y(d)).wait_recv()

    def core_send(d):
        mine = xt.at[x_rows(lax.rem(y - d + Y, Y) * 2 + core)]
        return rcopy(mine, mine, cs_s.at[d], cs_r.at[d], sibling)

    def core_recv(d):
        dst = xt.at[x_rows(lax.rem(y - d + Y, Y) * 2 + 1 - core)]
        rcopy(dst, dst, cs_s.at[d], cs_r.at[d], sibling).wait_recv()

    loads[0].wait()
    loads[1].wait()
    lax.fori_loop(0, H, mem_head, 0)
    loads[2].wait()
    for i in range(X):
        xown[i] = xin[:, i * F : (i + 1) * F].T
    pl.semaphore_wait(barrier, len(partners))
    send_stage1(MEM)
    own = pltpu.make_async_copy(xown.at[x], xt.at[x_rows(hd), x_cols(x)], xl)
    own.start()
    for d in (1, 3, 2):
        x_send(d).start()
    own.wait()
    for d in (1, 3, 2):
        y_send(x, d).start()
    loads[3].wait()
    loads[4].wait()
    lax.fori_loop(0, H, back_head, 0)
    send_stage1(BACK)
    for g in range(G):
        line_sums(MEM, g)
    for g in range(G):
        line_sums(BACK, g)
    lax.fori_loop(0, H // 2, inner_head, 0)
    for d in (1, 3, 2):
        x_recv(d)
        for e in (1, 3, 2):
            y_send(lax.rem(x - d + X, X), e).start()
    core_send(0).start()
    for g in range(G):
        scans(MEM, g)
    lax.fori_loop(H // 2, H, inner_head, 0)
    for g in range(G):
        for d in range(1, X):
            stage3_recv(MEM, g, d)
        lax.fori_loop(g * HG, (g + 1) * HG, query_head, 0)
    for g in range(G):
        scans(BACK, g)
    for g in range(G):
        for d in range(1, X):
            stage3_recv(BACK, g, d)
        lax.fori_loop(g * HG, (g + 1) * HG, key_value_head, 0)
    for d in (1, 3, 2):
        for xi in range(X):
            y_recv(xi, d)
        core_send(d).start()
    for d in range(Y):
        core_recv(d)

    def hops(j, way):
        odd = lax.rem(j, 2)
        return Z // 2 - 1 + odd if way == 0 else Z // 2 - odd

    def block(j, zt):
        return part[j, x_rows(lax.rem(zt + Z, Z))]

    def ring(j, way, s):
        zt = lax.rem(z + 1, Z) if way == 0 else lax.rem(z + Z - 1, Z)
        return rcopy(
            sb.at[j, way, s], rb.at[j, way, s], rs_s.at[j, way, s], rs_r.at[j, way, s], at_z(zt)
        )

    def target(j, way, s):
        left = hops(j, way) - s
        return z + left if way == 0 else z - left

    def weight_copy(j):
        return pltpu.make_async_copy(wout.at[j], weight_out.at[:, cols(j)], w_o.at[j])

    def slot(t, carry):
        @pl.when(t < H)
        def _():
            for d in range(1, X):
                qg_recv(t, d)
            for i in range(2):
                r = pl.ds(i * (FEATURES // 2), FEATURES // 2)
                part[t, r] = dot(xt[r, :], qg[t], 1, 0)
            for way in range(2):
                sb[t, way, 0] = block(t, target(t, way, 0)).astype(BF16)
                ring(t, way, 0).start()

        for s in range(1, Z // 2):
            j = t - s

            @pl.when((j >= 0) & (j < H))
            def _():
                for way in range(2):
                    @pl.when(s < hops(j, way))
                    def _():
                        ring(j, way, s - 1).wait_recv()
                        total = rb[j, way, s - 1].astype(F32) + block(j, target(j, way, s))
                        sb[j, way, s] = total.astype(BF16)
                        ring(j, way, s).start()

        last = t - Z // 2

        @pl.when(last >= 0)
        def _():
            total = block(last, z)
            for way in range(2):
                s = hops(last, way) - 1
                ring(last, way, s).wait_recv()
                total += rb[last, way, s].astype(F32)
            wout[last] = total
            weight_copy(last).start()

        return carry

    lax.fori_loop(0, H + Z // 2, slot, 0)

    def drain(h, carry):
        for d in range(1, X):
            qg_send(h, d).wait_send()
        for way in range(2):
            for s in range(Z // 2):
                @pl.when(s < hops(h, way))
                def _():
                    ring(h, way, s).wait_send()
        for c in kv_copies(h):
            c.wait()
        weight_copy(h).wait()
        return carry

    lax.fori_loop(0, H, drain, 0)
    for d in range(1, X):
        x_send(d).wait_send()
        for kind in range(2):
            for g in range(G):
                stage1(kind, g, d).wait_send()
                stage3(kind, g, d).wait_send()
    for d in range(1, Y):
        for xi in range(X):
            y_send(xi, d).wait_send()
    for d in range(Y):
        core_send(d).wait_send()
    for g in range(G):
        def up(zt, carry):
            stage2(MEM, g, zt).wait_send()
            return carry

        def down(zt, carry):
            stage2(BACK, g, zt).wait_send()
            return carry

        lax.fori_loop(z + 1, Z, up, 0)
        lax.fori_loop(0, z, down, 0)


def local(inputs, query, key_rows, value, grad_out, decay_power):
    dma = pltpu.SemaphoreType.DMA
    anywhere = pl.BlockSpec(memory_space=pl.ANY)
    return pl.pallas_call(
        kernel,
        out_shape=(
            jax.ShapeDtypeStruct((T, H * W), F32),
            jax.ShapeDtypeStruct((T, H * W), F32),
            jax.ShapeDtypeStruct((F, H * W), F32),
        ),
        in_specs=[anywhere] * 5 + [pl.BlockSpec(memory_space=pltpu.SMEM)],
        out_specs=(anywhere,) * 3,
        scratch_shapes=[
            pltpu.VMEM((T, X * F), BF16),
            pltpu.VMEM((T, H * W), BF16),
            pltpu.VMEM((T, H * W), BF16),
            pltpu.VMEM((T, H * W), BF16),
            pltpu.VMEM((T, H * W), BF16),
            pltpu.VMEM((X, F, T), BF16),
            pltpu.VMEM((FEATURES, X * T), BF16),
            pltpu.VMEM((H, W, W), F32),
            pltpu.VMEM((H, W, W), F32),
            pltpu.VMEM((2, X, H, Q, W), BF16),
            pltpu.VMEM((2, X, H, Q, W), BF16),
            pltpu.VMEM((2, H, Q, W), BF16),
            pltpu.VMEM((Z, H, Q, W), BF16),
            pltpu.VMEM((2, X, H, Q, W), BF16),
            pltpu.VMEM((2, X, H, Q, W), BF16),
            pltpu.VMEM((H, T, W), F32),
            pltpu.VMEM((H, T, W), F32),
            pltpu.VMEM((H, T, W), F32),
            pltpu.VMEM((H, X * T, W), BF16),
            pltpu.VMEM((H, FEATURES, W), F32),
            pltpu.VMEM((H, 2, Z // 2, F, W), BF16),
            pltpu.VMEM((H, 2, Z // 2, F, W), BF16),
            pltpu.VMEM((H, F, W), F32),
            dma((5,)),
            dma,
            dma((X - 1,)),
            dma((X - 1,)),
            dma((X, Y - 1)),
            dma((X, Y - 1)),
            dma((Y,)),
            dma((Y,)),
            dma((2, G, X - 1)),
            dma((2, G, X - 1)),
            dma((G, Z)),
            dma((G, Z)),
            dma((2, G, X - 1)),
            dma((2, G, X - 1)),
            dma((H, X - 1)),
            dma((H, X - 1)),
            dma((H, 2, Z // 2)),
            dma((H, 2, Z // 2)),
            dma((2, H)),
            dma((H,)),
        ],
        compiler_params=pltpu.CompilerParams(
            collective_id=0, has_side_effects=True, vmem_limit_bytes=60 * 2**20
        ),
        cost_estimate=pl.CostEstimate(
            flops=9 * 10**9, bytes_accessed=10 * 2**20, transcendentals=10**6
        ),
    )(inputs, query, key_rows, value, grad_out, decay_power)


def solution(mesh):
    placed = (P("ctx", "head"),) * 5 + (P(),)
    return jax.shard_map(
        local,
        mesh=mesh,
        in_specs=placed,
        out_specs=(P("ctx", "head"),) * 3,
        check_vma=False,
    )
```

```python
import math

import jax
import jax.numpy as jnp
from jax import lax
from jax.experimental import pallas as pl
from jax.experimental.pallas import tpu as pltpu
from jax.sharding import PartitionSpec as P

X, Z, Y = 4, 8, 4
W = 128
B = 256
T = 2 * B
H = 8
G = 2
HG = H // G
Q = W // X
F = 192
FEATURES = F * Z
MESH = pl.DeviceIdType.MESH
F32, BF16 = jnp.float32, jnp.bfloat16
MEM, BACK = 0, 1
LEAD = 2
FIRST = 2


def dot(a, b, ca, cb):
    return lax.dot_general(a, b, (((ca,), (cb,)), ((), ())), preferred_element_type=F32)


def rcopy(src, dst, ss, rs, dev):
    return pltpu.make_async_remote_copy(
        src_ref=src, dst_ref=dst, send_sem=ss, recv_sem=rs, device_id=dev, device_id_type=MESH
    )


def kernel(
    x_hbm, q_hbm, k_hbm, v_hbm, g_hbm, power,
    key_out, value_out, weight_out,
    xin, qv, kv, vv, gv, xown, xt, fades,
    bm0, bb1, memq, s1, lz, gz, out3, p3,
    qi, kg, vg, kgo, vgo, qg, part, sb, rb, wout,
    ld, xl, xs_s, xs_r, ys_s, ys_r, yf_s, yf_r, cs_s, cs_r,
    s1_s, s1_r, s2_s, s2_r, s3_s, s3_r, qg_s, qg_r, qf_s, qf_r, rs_s, rs_r, kv_o, w_o,
):
    ctx = lax.axis_index("ctx")
    hd = lax.axis_index("head")
    x, z = lax.rem(ctx, X), ctx // X
    y, core = hd // 2, lax.rem(hd, 2)

    def at_x(d):
        return (z * X + lax.rem(x + d, X), hd)

    def at_z(zt):
        return (zt * X + x, hd)

    def at_y(d):
        return (ctx, lax.rem(y + d, Y) * 2 + core)

    sibling = (ctx, y * 2 + 1 - core)

    loads = [
        pltpu.make_async_copy(src, dst, ld.at[i])
        for i, (src, dst) in enumerate(
            ((k_hbm, kv), (v_hbm, vv), (x_hbm, xin), (q_hbm, qv), (g_hbm, gv))
        )
    ]
    for c in loads:
        c.start()

    barrier = pltpu.get_barrier_semaphore()
    partners = (
        [at_x(d) for d in range(1, X)]
        + [at_z(lax.rem(z + d, Z)) for d in range(1, Z)]
        + [at_y(d) for d in range(1, Y)]
        + [sibling]
    )
    for dev in partners:
        pl.semaphore_signal(barrier, inc=1, device_id=dev, device_id_type=MESH)

    def rate_of(h):
        return power[hd * H + h].astype(F32) * (math.log(2.0) / (4.0 * T * X * Z))

    def decay(rate, count):
        return jnp.exp(jnp.full((1, W), -rate * count, F32))

    def rows():
        return lax.broadcasted_iota(jnp.int32, (B, W), 0).astype(F32)

    def cols(h):
        if isinstance(h, int):
            return pl.ds(h * W, W)
        return pl.ds(pl.multiple_of(h * W, W), W)

    for h in range(H):
        for i, count in enumerate((T, T * X)):
            fades[i, h] = jnp.exp(jnp.full((8, W), -rate_of(h) * float(count), F32))

    def keep(i, g):
        return fades[i, g * HG : (g + 1) * HG, 0:1]

    def mem_head(h, carry):
        rate = rate_of(h)
        tail = jnp.exp(-rate * ((B - 1.0) - rows()))
        sums = []
        for b in range(2):
            r = pl.ds(b * B, B)
            low = (kv[r, cols(h)].astype(F32) * tail).astype(BF16)
            sums.append(dot(low, vv[r, cols(h)], 0, 0))
        bm0[h] = sums[0]
        m = (decay(rate, float(B)) * sums[0] + sums[1]).astype(BF16)
        for i in range(X):
            memq[MEM, i, h] = m[i * Q : (i + 1) * Q]
        return carry

    def back_head(h, carry):
        rate = rate_of(h)
        lead = jnp.exp(-rate * rows())
        sums = []
        for b in range(2):
            r = pl.ds(b * B, B)
            low = (qv[r, cols(h)].astype(F32) * lead).astype(BF16)
            sums.append(dot(low, gv[r, cols(h)], 0, 0))
        bb1[h] = sums[1]
        m = (sums[0] + decay(rate, float(B)) * sums[1]).astype(BF16)
        for i in range(X):
            memq[BACK, i, h] = m[i * Q : (i + 1) * Q]
        return carry

    def heads(g):
        return pl.ds(g * HG, HG)

    def stage1(kind, g, d):
        xt_to = lax.rem(x + d, X)
        return rcopy(
            memq.at[kind, xt_to, heads(g)], s1.at[kind, x, heads(g)],
            s1_s.at[kind, g, d - 1], s1_r.at[kind, g, d - 1], at_x(d),
        )

    def stage1_recv(kind, g, d):
        xf = lax.rem(x - d + X, X)
        dst = s1.at[kind, xf, heads(g)]
        rcopy(dst, dst, s1_s.at[kind, g, d - 1], s1_r.at[kind, g, d - 1], at_x(d)).wait_recv()

    def send_stage1(kind):
        s1[kind, x] = memq[kind, x]
        for g in range(G):
            for d in (1, 3, 2):
                stage1(kind, g, d).start()

    def stage2(kind, g, zt):
        return rcopy(
            lz.at[kind, heads(g)], gz.at[z, heads(g)], s2_s.at[g, zt], s2_r.at[g, z], at_z(zt)
        )

    def line_sums(kind, g):
        for d in range(1, X):
            stage1_recv(kind, g, d)

        d = keep(0, g)
        total = None
        for xi in range(X) if kind == MEM else range(X - 1, -1, -1):
            term = s1[kind, xi, g * HG : (g + 1) * HG].astype(F32)
            total = term if total is None else total * d + term
        lz[kind, g * HG : (g + 1) * HG] = total.astype(BF16)

        def send(i, carry):
            zt = z + 1 + i if kind == MEM else z - 1 - i
            stage2(kind, g, zt).start()
            return carry

        lax.fori_loop(0, Z - 1 - z if kind == MEM else z, send, 0)

    def stage3(kind, g, d):
        xt_to = lax.rem(x + d, X)
        return rcopy(
            out3.at[kind, xt_to, heads(g)], p3.at[kind, x, heads(g)],
            s3_s.at[kind, g, d - 1], s3_r.at[kind, g, d - 1], at_x(d),
        )

    def stage3_recv(kind, g, d):
        xf = lax.rem(x - d + X, X)
        dst = p3.at[kind, xf, heads(g)]
        rcopy(dst, dst, s3_s.at[kind, g, d - 1], s3_r.at[kind, g, d - 1], at_x(d)).wait_recv()

    def scans(kind, g):
        count = z if kind == MEM else Z - 1 - z

        def source(i):
            return i if kind == MEM else Z - 1 - i

        line_fade = keep(1, g)

        def add(i, total):
            dst = gz.at[source(i), heads(g)]
            rcopy(dst, dst, s2_s.at[g, 0], s2_r.at[g, source(i)], at_z(source(i))).wait_recv()
            return total * line_fade + gz[source(i), g * HG : (g + 1) * HG].astype(F32)

        run = lax.fori_loop(0, count, add, jnp.zeros((HG, Q, W), F32))
        d = keep(0, g)
        for xi in range(X) if kind == MEM else range(X - 1, -1, -1):
            out3[kind, xi, g * HG : (g + 1) * HG] = run.astype(BF16)
            run = run * d + s1[kind, xi, g * HG : (g + 1) * HG].astype(F32)
        p3[kind, x, heads(g)] = out3[kind, x, heads(g)]
        for d in (1, 3, 2):
            stage3(kind, g, d).start()

    def inner_head(h, carry):
        rate = rate_of(h)
        t = lax.broadcasted_iota(jnp.int32, (B, B), 0)
        s = lax.broadcasted_iota(jnp.int32, (B, B), 1)
        gap = (t - s).astype(F32)
        fade = jnp.where(gap >= 0.0, jnp.exp(-rate * jnp.maximum(gap, 0.0)), 0.0)
        turned = jnp.where(gap <= 0.0, jnp.exp(rate * jnp.minimum(gap, 0.0)), 0.0)
        for b in range(2):
            r = pl.ds(b * B, B)
            qh, kh, vh, gh = (a[r, cols(h)] for a in (qv, kv, vv, gv))
            sa = (dot(gh, vh, 1, 1) * fade).astype(BF16)
            qi[h, r] = dot(sa, kh, 1, 0)
            sat = (dot(vh, gh, 1, 1) * turned).astype(BF16)
            kg[h, r] = dot(sat, qh, 1, 0)
            sbt = (dot(kh, qh, 1, 1) * turned).astype(BF16)
            vg[h, r] = dot(sbt, gh, 1, 0)
        return carry

    def line(xi, half=None):
        if half is None:
            return pl.ds(pl.multiple_of(lax.rem(xi + X, X) * T, T), T)
        return pl.ds(pl.multiple_of(lax.rem(xi + X, X) * T + half * B, B), B)

    def qg_send(h, way):
        mine = qg.at[h, line(x)]
        return rcopy(mine, mine, qg_s.at[h, way], qg_r.at[h, way], at_x(X - 1 if way else 1))

    def qg_recv(h, way):
        dst = qg.at[h, line(x + 1 if way else x - 1)]
        rcopy(dst, dst, qg_s.at[h, way], qg_r.at[h, way], at_x(1)).wait_recv()

    def qg_pass(h, way):
        got = qg.at[h, line(x + 1 if way else x - 1, way)]
        return rcopy(got, got, qf_s.at[h, way], qf_r.at[h, way], at_x(X - 1 if way else 1))

    def qg_pass_recv(h, way):
        dst = qg.at[h, line(x + 2, way)]
        rcopy(dst, dst, qf_s.at[h, way], qf_r.at[h, way], at_x(1)).wait_recv()

    def query_head(h, carry):
        rate = rate_of(h)
        lead = jnp.exp(-rate * (rows() + 1.0))
        prefix = p3[MEM, :, h].reshape(W, W)
        starts = (prefix, (decay(rate, float(B)) * prefix.astype(F32) + bm0[h]).astype(BF16))
        for b in range(2):
            r = pl.ds(b * B, B)
            whole = qi[h, r] + lead * dot(gv[r, cols(h)], starts[b], 1, 1)
            qg[h, line(x, b)] = whole.astype(BF16)
        if h < LEAD:
            for way in range(2):
                qg_send(h, way).start()

        return carry

    def kv_copies(h):
        return (
            pltpu.make_async_copy(kgo.at[h], key_out.at[:, cols(h)], kv_o.at[0, h]),
            pltpu.make_async_copy(vgo.at[h], value_out.at[:, cols(h)], kv_o.at[1, h]),
        )

    def key_value_head(h, carry):
        rate = rate_of(h)
        fall = jnp.exp(-rate * (float(B) - rows()))
        suffix = p3[BACK, :, h].reshape(W, W)
        finishes = ((decay(rate, float(B)) * suffix.astype(F32) + bb1[h]).astype(BF16), suffix)
        for b in range(2):
            r = pl.ds(b * B, B)
            kgo[h, r] = (kg[h, r] + fall * dot(vv[r, cols(h)], finishes[b], 1, 1)).astype(BF16)
            vgo[h, r] = (vg[h, r] + fall * dot(kv[r, cols(h)], finishes[b], 1, 0)).astype(BF16)
        for c in kv_copies(h):
            c.start()
        return carry

    def x_rows(owner):
        return pl.ds(pl.multiple_of(owner * F, F), F)

    def x_cols(xi):
        return pl.ds(pl.multiple_of(xi * T, T), T)

    def x_send(d):
        return rcopy(
            xown.at[x_rows(lax.rem(x + d, X))], xt.at[x_rows(hd), x_cols(x)],
            xs_s.at[d - 1], xs_r.at[d - 1], at_x(d),
        )

    def x_recv(d):
        xf = lax.rem(x - d + X, X)
        dst = xt.at[x_rows(hd), x_cols(xf)]
        rcopy(dst, dst, xs_s.at[d - 1], xs_r.at[d - 1], at_x(d)).wait_recv()

    def y_part(owner_y, xi, half=None):
        owner = lax.rem(owner_y + Y, Y) * 2 + core
        if half is None:
            return xt.at[x_rows(owner), x_cols(xi)]
        return xt.at[pl.ds(pl.multiple_of(owner * F + half * (F // 2), F // 2), F // 2), x_cols(xi)]

    def y_send(xi, way):
        mine = y_part(y, xi)
        return rcopy(mine, mine, ys_s.at[xi, way], ys_r.at[xi, way], at_y(Y - 1 if way else 1))

    def y_recv(xi, way):
        dst = y_part(y + 1 if way else y - 1, xi)
        rcopy(dst, dst, ys_s.at[xi, way], ys_r.at[xi, way], at_y(1)).wait_recv()

    def y_pass(xi, way):
        got = y_part(y + 1 if way else y - 1, xi, way)
        return rcopy(got, got, yf_s.at[xi, way], yf_r.at[xi, way], at_y(Y - 1 if way else 1))

    def y_pass_recv(xi, way):
        dst = y_part(y + 2, xi, way)
        rcopy(dst, dst, yf_s.at[xi, way], yf_r.at[xi, way], at_y(1)).wait_recv()

    def y_start(xi):
        for way in range(2):
            y_send(xi, way).start()

    def y_forward(xi):
        for way in range(2):
            y_recv(xi, way)
            y_pass(xi, way).start()

    def core_send(d):
        mine = xt.at[x_rows(lax.rem(y - d + Y, Y) * 2 + core)]
        return rcopy(mine, mine, cs_s.at[d], cs_r.at[d], sibling)

    def core_recv(d):
        dst = xt.at[x_rows(lax.rem(y - d + Y, Y) * 2 + 1 - core)]
        rcopy(dst, dst, cs_s.at[d], cs_r.at[d], sibling).wait_recv()

    loads[0].wait()
    loads[1].wait()
    for h in range(H):
        mem_head(h, 0)
    pl.semaphore_wait(barrier, len(partners))
    send_stage1(MEM)
    loads[2].wait()
    for i in range(X * F // W):
        xown[i * W : (i + 1) * W] = xin[:, i * W : (i + 1) * W].T
    own = pltpu.make_async_copy(xown.at[x_rows(x)], xt.at[x_rows(hd), x_cols(x)], xl)
    own.start()
    for d in (1, 3, 2):
        x_send(d).start()
    own.wait()
    y_start(x)
    loads[3].wait()
    loads[4].wait()
    for h in range(H):
        back_head(h, 0)
    send_stage1(BACK)
    for g in range(G):
        line_sums(MEM, g)
    lax.fori_loop(0, 3, inner_head, 0)
    for d in (1, 3):
        x_recv(d)
        y_start(lax.rem(x - d + X, X))
    y_forward(x)
    lax.fori_loop(3, 6, inner_head, 0)
    x_recv(2)
    y_start(lax.rem(x + 2, X))
    core_send(0).start()
    for g in range(G):
        scans(MEM, g)
    y_forward(lax.rem(x + 3, X))
    for g in range(G):
        line_sums(BACK, g)
    lax.fori_loop(6, H, inner_head, 0)
    for g in range(G):
        for d in range(1, X):
            stage3_recv(MEM, g, d)
        for h in range(g * HG, (g + 1) * HG):
            query_head(h, 0)
        y_forward(lax.rem(x + 1 + g, X))

    def keys_values(g):
        for d in range(1, X):
            stage3_recv(BACK, g, d)
        lax.fori_loop(g * HG, (g + 1) * HG, key_value_head, 0)

    def inputs_near():
        for d in (1, 3):
            core_send(d).start()

    def inputs_far():
        for xi in range(X):
            for way in range(2):
                y_pass_recv(xi, way)
        core_send(2).start()

    def inputs_all():
        for d in range(Y):
            core_recv(d)

    def hops(j, way):
        odd = lax.rem(j, 2)
        return Z // 2 - 1 + odd if way == 0 else Z // 2 - odd

    def block(j, zt):
        return part[j, x_rows(lax.rem(zt + Z, Z))]

    def ring(j, way, s):
        zt = lax.rem(z + 1, Z) if way == 0 else lax.rem(z + Z - 1, Z)
        return rcopy(
            sb.at[j, way, s], rb.at[j, way, s], rs_s.at[j, way, s], rs_r.at[j, way, s], at_z(zt)
        )

    def target(j, way, s):
        left = hops(j, way) - s
        return z + left if way == 0 else z - left

    def weight_copy(j):
        return pltpu.make_async_copy(wout.at[j], weight_out.at[:, cols(j)], w_o.at[j])

    def product(j, carry):
        for way in range(2):
            qg_pass_recv(j, way)
        for i in range(2):
            r = pl.ds(i * (FEATURES // 2), FEATURES // 2)
            part[j, r] = dot(xt[r, :], qg[j], 1, 0)
        for way in range(2):
            sb[j, way, 0] = block(j, target(j, way, 0)).astype(BF16)
            ring(j, way, 0).start()
        return carry

    def level(s):
        def one(j, carry):
            for way in range(2):
                @pl.when(s < hops(j, way))
                def _():
                    ring(j, way, s - 1).wait_recv()
                    total = rb[j, way, s - 1].astype(F32) + block(j, target(j, way, s))
                    sb[j, way, s] = total.astype(BF16)
                    ring(j, way, s).start()

            return carry

        return one

    def finish(j, carry):
        total = block(j, z)
        for way in range(2):
            s = hops(j, way) - 1
            ring(j, way, s).wait_recv()
            total += rb[j, way, s].astype(F32)
        wout[j] = total
        weight_copy(j).start()
        return carry

    def slot(t, carry):
        @pl.when(t + LEAD < H)
        def _():
            for way in range(2):
                qg_send(t + LEAD, way).start()

        @pl.when(t < H)
        def _():
            for way in range(2):
                qg_recv(t, way)
                qg_pass(t, way).start()

        @pl.when(t == 0)
        def _():
            inputs_near()

        @pl.when(t == FIRST - 1)
        def _():
            inputs_far()
            for g in range(G):
                scans(BACK, g)

        @pl.when(t == FIRST)
        def _():
            inputs_all()

        for s in range(Z // 2, -1, -1):
            u = t - 1 - s
            first = (u == FIRST - 1).astype(jnp.int32)
            low = u - first * (FIRST - 1)
            high = jnp.where((u >= FIRST - 1) & (u < H), u + 1, low)
            step = product if s == 0 else finish if s == Z // 2 else level(s)
            lax.fori_loop(low, high, step, 0)

        for g in range(G):
            @pl.when(t == FIRST + 1 + g)
            def _():
                keys_values(g)

        return carry

    lax.fori_loop(0, H + 1 + Z // 2, slot, 0)

    def drain(h, carry):
        for way in range(2):
            qg_send(h, way).wait_send()
            qg_pass(h, way).wait_send()
        for way in range(2):
            for s in range(Z // 2):
                @pl.when(s < hops(h, way))
                def _():
                    ring(h, way, s).wait_send()
        for c in kv_copies(h):
            c.wait()
        weight_copy(h).wait()
        return carry

    lax.fori_loop(0, H, drain, 0)
    for d in range(1, X):
        x_send(d).wait_send()
        for kind in range(2):
            for g in range(G):
                stage1(kind, g, d).wait_send()
                stage3(kind, g, d).wait_send()
    for xi in range(X):
        for way in range(2):
            y_send(xi, way).wait_send()
            y_pass(xi, way).wait_send()
    for d in range(Y):
        core_send(d).wait_send()
    for g in range(G):
        def up(zt, carry):
            stage2(MEM, g, zt).wait_send()
            return carry

        def down(zt, carry):
            stage2(BACK, g, zt).wait_send()
            return carry

        lax.fori_loop(z + 1, Z, up, 0)
        lax.fori_loop(0, z, down, 0)


def local(inputs, query, key_rows, value, grad_out, decay_power):
    dma = pltpu.SemaphoreType.DMA
    anywhere = pl.BlockSpec(memory_space=pl.ANY)
    key_grad, value_grad, weight_grad = pl.pallas_call(
        kernel,
        out_shape=(
            jax.ShapeDtypeStruct((T, H * W), BF16),
            jax.ShapeDtypeStruct((T, H * W), BF16),
            jax.ShapeDtypeStruct((F, H * W), F32),
        ),
        in_specs=[anywhere] * 5 + [pl.BlockSpec(memory_space=pltpu.SMEM)],
        out_specs=(anywhere,) * 3,
        scratch_shapes=[
            pltpu.VMEM((T, X * F), BF16),
            pltpu.VMEM((T, H * W), BF16),
            pltpu.VMEM((T, H * W), BF16),
            pltpu.VMEM((T, H * W), BF16),
            pltpu.VMEM((T, H * W), BF16),
            pltpu.VMEM((X * F, T), BF16),
            pltpu.VMEM((FEATURES, X * T), BF16),
            pltpu.VMEM((2, H, 8, W), F32),
            pltpu.VMEM((H, W, W), F32),
            pltpu.VMEM((H, W, W), F32),
            pltpu.VMEM((2, X, H, Q, W), BF16),
            pltpu.VMEM((2, X, H, Q, W), BF16),
            pltpu.VMEM((2, H, Q, W), BF16),
            pltpu.VMEM((Z, H, Q, W), BF16),
            pltpu.VMEM((2, X, H, Q, W), BF16),
            pltpu.VMEM((2, X, H, Q, W), BF16),
            pltpu.VMEM((H, T, W), F32),
            pltpu.VMEM((H, T, W), F32),
            pltpu.VMEM((H, T, W), F32),
            pltpu.VMEM((H, T, W), BF16),
            pltpu.VMEM((H, T, W), BF16),
            pltpu.VMEM((H, X * T, W), BF16),
            pltpu.VMEM((H, FEATURES, W), F32),
            pltpu.VMEM((H, 2, Z // 2, F, W), BF16),
            pltpu.VMEM((H, 2, Z // 2, F, W), BF16),
            pltpu.VMEM((H, F, W), F32),
            dma((5,)),
            dma,
            dma((X - 1,)),
            dma((X - 1,)),
            dma((X, 2)),
            dma((X, 2)),
            dma((X, 2)),
            dma((X, 2)),
            dma((Y,)),
            dma((Y,)),
            dma((2, G, X - 1)),
            dma((2, G, X - 1)),
            dma((G, Z)),
            dma((G, Z)),
            dma((2, G, X - 1)),
            dma((2, G, X - 1)),
            dma((H, 2)),
            dma((H, 2)),
            dma((H, 2)),
            dma((H, 2)),
            dma((H, 2, Z // 2)),
            dma((H, 2, Z // 2)),
            dma((2, H)),
            dma((H,)),
        ],
        compiler_params=pltpu.CompilerParams(
            collective_id=0, has_side_effects=True, vmem_limit_bytes=60 * 2**20
        ),
        cost_estimate=pl.CostEstimate(
            flops=9 * 10**9, bytes_accessed=10 * 2**20, transcendentals=10**6
        ),
    )(inputs, query, key_rows, value, grad_out, decay_power)
    return key_grad.astype(F32), value_grad.astype(F32), weight_grad


def solution(mesh):
    placed = (P("ctx", "head"),) * 5 + (P(),)
    return jax.shard_map(
        local,
        mesh=mesh,
        in_specs=placed,
        out_specs=(P("ctx", "head"),) * 3,
        check_vma=False,
    )
```

```python
import math

import jax
import jax.numpy as jnp
from jax import lax
from jax.experimental import pallas as pl
from jax.experimental.pallas import tpu as pltpu
from jax.sharding import PartitionSpec as P

X, Z, Y = 4, 8, 4
W = 128
B = 256
T = 2 * B
H = 8
G = 2
HG = H // G
Q = W // X
F = 192
FEATURES = F * Z
MESH = pl.DeviceIdType.MESH
F32, BF16 = jnp.float32, jnp.bfloat16
MEM, BACK = 0, 1
LEAD = 3
LAG = 2


def dot(a, b, ca, cb):
    return lax.dot_general(a, b, (((ca,), (cb,)), ((), ())), preferred_element_type=F32)


def rcopy(src, dst, ss, rs, dev):
    return pltpu.make_async_remote_copy(
        src_ref=src, dst_ref=dst, send_sem=ss, recv_sem=rs, device_id=dev, device_id_type=MESH
    )


def kernel(
    x_hbm, q_hbm, k_hbm, v_hbm, g_hbm, power,
    key_out, value_out, weight_out,
    xin, qv, kv, vv, gv, xown, xt, fades,
    bm0, bb1, memq, s1, lz, gz, out3, p3,
    qi, kgo, vgo, qg, part, sb, rb, wout,
    ld, xl, xs_s, xs_r, ys_s, ys_r, yf_s, yf_r, cs_s, cs_r,
    s1_s, s1_r, s2_s, s2_r, s3_s, s3_r, qg_s, qg_r, qf_s, qf_r, rs_s, rs_r, kv_o, w_o,
):
    ctx = lax.axis_index("ctx")
    hd = lax.axis_index("head")
    x, z = lax.rem(ctx, X), ctx // X
    y, core = hd // 2, lax.rem(hd, 2)

    def at_x(d):
        return (z * X + lax.rem(x + d, X), hd)

    def at_z(zt):
        return (zt * X + x, hd)

    def at_y(d):
        return (ctx, lax.rem(y + d, Y) * 2 + core)

    sibling = (ctx, y * 2 + 1 - core)

    loads = [
        pltpu.make_async_copy(src, dst, ld.at[i])
        for i, (src, dst) in enumerate(
            ((x_hbm, xin), (k_hbm, kv), (v_hbm, vv), (q_hbm, qv), (g_hbm, gv))
        )
    ]
    for c in loads:
        c.start()

    barrier = pltpu.get_barrier_semaphore()
    partners = (
        [at_x(d) for d in range(1, X)]
        + [at_z(lax.rem(z + d, Z)) for d in range(1, Z)]
        + [at_y(d) for d in range(1, Y)]
        + [sibling]
    )
    for dev in partners:
        pl.semaphore_signal(barrier, inc=1, device_id=dev, device_id_type=MESH)

    def rate_of(h):
        return power[hd * H + h].astype(F32) * (math.log(2.0) / (4.0 * T * X * Z))

    def decay(rate, count):
        return jnp.exp(jnp.full((1, W), -rate * count, F32))

    def rows():
        return lax.broadcasted_iota(jnp.int32, (B, W), 0).astype(F32)

    def cols(h):
        if isinstance(h, int):
            return pl.ds(h * W, W)
        return pl.ds(pl.multiple_of(h * W, W), W)

    for h in range(H):
        for i, count in enumerate((T, T * X)):
            fades[i, h] = jnp.exp(jnp.full((8, W), -rate_of(h) * float(count), F32))

    def keep(i, g):
        return fades[i, g * HG : (g + 1) * HG, 0:1]

    def mem_head(h, carry):
        rate = rate_of(h)
        tail = jnp.exp(-rate * ((B - 1.0) - rows()))
        sums = []
        for b in range(2):
            r = pl.ds(b * B, B)
            low = (kv[r, cols(h)].astype(F32) * tail).astype(BF16)
            sums.append(dot(low, vv[r, cols(h)], 0, 0))
        bm0[h] = sums[0]
        m = (decay(rate, float(B)) * sums[0] + sums[1]).astype(BF16)
        for i in range(X):
            memq[MEM, i, h] = m[i * Q : (i + 1) * Q]
        return carry

    def back_head(h, carry):
        rate = rate_of(h)
        lead = jnp.exp(-rate * rows())
        sums = []
        for b in range(2):
            r = pl.ds(b * B, B)
            low = (qv[r, cols(h)].astype(F32) * lead).astype(BF16)
            sums.append(dot(low, gv[r, cols(h)], 0, 0))
        bb1[h] = sums[1]
        m = (sums[0] + decay(rate, float(B)) * sums[1]).astype(BF16)
        for i in range(X):
            memq[BACK, i, h] = m[i * Q : (i + 1) * Q]
        return carry

    def heads(g):
        return pl.ds(g * HG, HG)

    def stage1(kind, g, d):
        xt_to = lax.rem(x + d, X)
        return rcopy(
            memq.at[kind, xt_to, heads(g)], s1.at[kind, x, heads(g)],
            s1_s.at[kind, g, d - 1], s1_r.at[kind, g, d - 1], at_x(d),
        )

    def stage1_recv(kind, g, d):
        xf = lax.rem(x - d + X, X)
        dst = s1.at[kind, xf, heads(g)]
        rcopy(dst, dst, s1_s.at[kind, g, d - 1], s1_r.at[kind, g, d - 1], at_x(d)).wait_recv()

    def send_stage1(kind):
        s1[kind, x] = memq[kind, x]
        for g in range(G):
            for d in (1, 3, 2):
                stage1(kind, g, d).start()

    def stage2(kind, g, zt):
        return rcopy(
            lz.at[kind, heads(g)], gz.at[z, heads(g)], s2_s.at[g, zt], s2_r.at[g, z], at_z(zt)
        )

    def line_sums(kind, g):
        for d in range(1, X):
            stage1_recv(kind, g, d)

        d = keep(0, g)
        total = None
        for xi in range(X) if kind == MEM else range(X - 1, -1, -1):
            term = s1[kind, xi, g * HG : (g + 1) * HG].astype(F32)
            total = term if total is None else total * d + term
        lz[kind, g * HG : (g + 1) * HG] = total.astype(BF16)

        def send(i, carry):
            zt = z + 1 + i if kind == MEM else z - 1 - i
            stage2(kind, g, zt).start()
            return carry

        lax.fori_loop(0, Z - 1 - z if kind == MEM else z, send, 0)

    def stage3(kind, g, d):
        xt_to = lax.rem(x + d, X)
        return rcopy(
            out3.at[kind, xt_to, heads(g)], p3.at[kind, x, heads(g)],
            s3_s.at[kind, g, d - 1], s3_r.at[kind, g, d - 1], at_x(d),
        )

    def stage3_recv(kind, g, d):
        xf = lax.rem(x - d + X, X)
        dst = p3.at[kind, xf, heads(g)]
        rcopy(dst, dst, s3_s.at[kind, g, d - 1], s3_r.at[kind, g, d - 1], at_x(d)).wait_recv()

    def scans(kind, g):
        count = z if kind == MEM else Z - 1 - z

        def source(i):
            return i if kind == MEM else Z - 1 - i

        line_fade = keep(1, g)

        def add(i, total):
            dst = gz.at[source(i), heads(g)]
            rcopy(dst, dst, s2_s.at[g, 0], s2_r.at[g, source(i)], at_z(source(i))).wait_recv()
            return total * line_fade + gz[source(i), g * HG : (g + 1) * HG].astype(F32)

        run = lax.fori_loop(0, count, add, jnp.zeros((HG, Q, W), F32))
        d = keep(0, g)
        for xi in range(X) if kind == MEM else range(X - 1, -1, -1):
            out3[kind, xi, g * HG : (g + 1) * HG] = run.astype(BF16)
            run = run * d + s1[kind, xi, g * HG : (g + 1) * HG].astype(F32)
        p3[kind, x, heads(g)] = out3[kind, x, heads(g)]
        for d in (1, 3, 2):
            stage3(kind, g, d).start()

    def gaps():
        t = lax.broadcasted_iota(jnp.int32, (B, B), 0)
        s = lax.broadcasted_iota(jnp.int32, (B, B), 1)
        return (t - s).astype(F32)

    def inner_head(h, carry):
        gap = gaps()
        fade = jnp.where(gap >= 0.0, jnp.exp(-rate_of(h) * jnp.maximum(gap, 0.0)), 0.0)
        for b in range(2):
            r = pl.ds(b * B, B)
            sa = (dot(gv[r, cols(h)], vv[r, cols(h)], 1, 1) * fade).astype(BF16)
            qi[h, r] = dot(sa, kv[r, cols(h)], 1, 0)
        return carry

    def line(xi, half=None):
        if half is None:
            return pl.ds(pl.multiple_of(lax.rem(xi + X, X) * T, T), T)
        return pl.ds(pl.multiple_of(lax.rem(xi + X, X) * T + half * B, B), B)

    def qg_send(h, way):
        mine = qg.at[h, line(x)]
        return rcopy(mine, mine, qg_s.at[h, way], qg_r.at[h, way], at_x(X - 1 if way else 1))

    def qg_recv(h, way):
        dst = qg.at[h, line(x + 1 if way else x - 1)]
        rcopy(dst, dst, qg_s.at[h, way], qg_r.at[h, way], at_x(1)).wait_recv()

    def qg_pass(h, way):
        got = qg.at[h, line(x + 1 if way else x - 1, way)]
        return rcopy(got, got, qf_s.at[h, way], qf_r.at[h, way], at_x(X - 1 if way else 1))

    def qg_pass_recv(h, way):
        dst = qg.at[h, line(x + 2, way)]
        rcopy(dst, dst, qf_s.at[h, way], qf_r.at[h, way], at_x(1)).wait_recv()

    def query_head(h, carry):
        rate = rate_of(h)
        lead = jnp.exp(-rate * (rows() + 1.0))
        prefix = p3[MEM, :, h].reshape(W, W)
        starts = (prefix, (decay(rate, float(B)) * prefix.astype(F32) + bm0[h]).astype(BF16))
        for b in range(2):
            r = pl.ds(b * B, B)
            whole = qi[h, r] + lead * dot(gv[r, cols(h)], starts[b], 1, 1)
            qg[h, line(x, b)] = whole.astype(BF16)
        if h < LEAD:
            for way in range(2):
                qg_send(h, way).start()

        return carry

    def kv_copies(h):
        return (
            pltpu.make_async_copy(kgo.at[h], key_out.at[:, cols(h)], kv_o.at[0, h]),
            pltpu.make_async_copy(vgo.at[h], value_out.at[:, cols(h)], kv_o.at[1, h]),
        )

    def key_value_head(h, carry):
        rate = rate_of(h)
        gap = gaps()
        turned = jnp.where(gap <= 0.0, jnp.exp(rate * jnp.minimum(gap, 0.0)), 0.0)
        fall = jnp.exp(-rate * (float(B) - rows()))
        suffix = p3[BACK, :, h].reshape(W, W)
        finishes = ((decay(rate, float(B)) * suffix.astype(F32) + bb1[h]).astype(BF16), suffix)
        for b in range(2):
            r = pl.ds(b * B, B)
            qh, kh, vh, gh = (a[r, cols(h)] for a in (qv, kv, vv, gv))
            sat = (dot(vh, gh, 1, 1) * turned).astype(BF16)
            kgo[h, r] = (dot(sat, qh, 1, 0) + fall * dot(vh, finishes[b], 1, 1)).astype(BF16)
            sbt = (dot(kh, qh, 1, 1) * turned).astype(BF16)
            vgo[h, r] = (dot(sbt, gh, 1, 0) + fall * dot(kh, finishes[b], 1, 0)).astype(BF16)
        for c in kv_copies(h):
            c.start()
        return carry

    def x_rows(owner):
        return pl.ds(pl.multiple_of(owner * F, F), F)

    def x_cols(xi):
        return pl.ds(pl.multiple_of(xi * T, T), T)

    def x_send(d):
        return rcopy(
            xown.at[x_rows(lax.rem(x + d, X))], xt.at[x_rows(hd), x_cols(x)],
            xs_s.at[d - 1], xs_r.at[d - 1], at_x(d),
        )

    def x_recv(d):
        xf = lax.rem(x - d + X, X)
        dst = xt.at[x_rows(hd), x_cols(xf)]
        rcopy(dst, dst, xs_s.at[d - 1], xs_r.at[d - 1], at_x(d)).wait_recv()

    def y_part(owner_y, xi, half=None):
        owner = lax.rem(owner_y + Y, Y) * 2 + core
        if half is None:
            return xt.at[x_rows(owner), x_cols(xi)]
        return xt.at[pl.ds(pl.multiple_of(owner * F + half * (F // 2), F // 2), F // 2), x_cols(xi)]

    def y_send(xi, way):
        mine = y_part(y, xi)
        return rcopy(mine, mine, ys_s.at[xi, way], ys_r.at[xi, way], at_y(Y - 1 if way else 1))

    def y_recv(xi, way):
        dst = y_part(y + 1 if way else y - 1, xi)
        rcopy(dst, dst, ys_s.at[xi, way], ys_r.at[xi, way], at_y(1)).wait_recv()

    def y_pass(xi, way):
        got = y_part(y + 1 if way else y - 1, xi, way)
        return rcopy(got, got, yf_s.at[xi, way], yf_r.at[xi, way], at_y(Y - 1 if way else 1))

    def y_pass_recv(xi, way):
        dst = y_part(y + 2, xi, way)
        rcopy(dst, dst, yf_s.at[xi, way], yf_r.at[xi, way], at_y(1)).wait_recv()

    def y_start(xi):
        for way in range(2):
            y_send(xi, way).start()

    def y_forward(xi):
        for way in range(2):
            y_recv(xi, way)
            y_pass(xi, way).start()

    def y_far(xi):
        mine = y_part(y, xi)
        return rcopy(mine, mine, yf_s.at[xi, 0], yf_r.at[xi, 0], at_y(2))

    def y_far_recv(xi):
        dst = y_part(y + 2, xi)
        rcopy(dst, dst, yf_s.at[xi, 0], yf_r.at[xi, 0], at_y(2)).wait_recv()

    def core_send(d):
        mine = xt.at[x_rows(lax.rem(y - d + Y, Y) * 2 + core)]
        return rcopy(mine, mine, cs_s.at[d], cs_r.at[d], sibling)

    def core_recv(d):
        dst = xt.at[x_rows(lax.rem(y - d + Y, Y) * 2 + 1 - core)]
        rcopy(dst, dst, cs_s.at[d], cs_r.at[d], sibling).wait_recv()

    loads[0].wait()
    for i in range(X * F // W):
        xown[i * W : (i + 1) * W] = xin[:, i * W : (i + 1) * W].T
    loads[1].wait()
    loads[2].wait()
    for h in range(H):
        mem_head(h, 0)
    pl.semaphore_wait(barrier, len(partners))
    send_stage1(MEM)
    own = pltpu.make_async_copy(xown.at[x_rows(x)], xt.at[x_rows(hd), x_cols(x)], xl)
    own.start()
    for d in (1, 3):
        x_send(d).start()
    own.wait()
    y_start(x)
    loads[3].wait()
    loads[4].wait()
    for h in range(H):
        back_head(h, 0)
    line_sums(MEM, 0)
    lax.fori_loop(0, H // 2, inner_head, 0)
    x_send(2).start()
    y_forward(x)
    for d in (1, 3):
        x_recv(d)
        y_start(lax.rem(x - d + X, X))
    line_sums(MEM, 1)
    send_stage1(BACK)
    lax.fori_loop(H // 2, H, inner_head, 0)
    x_recv(2)
    y_start(lax.rem(x + 2, X))
    y_far(lax.rem(x + 2, X)).start()
    core_send(0).start()
    scans(MEM, 0)
    y_forward(lax.rem(x + 3, X))
    y_forward(lax.rem(x + 1, X))

    def queries(g):
        for d in range(1, X):
            stage3_recv(MEM, g, d)
        for h in range(g * HG, (g + 1) * HG):
            query_head(h, 0)

    def keys_values(g):
        for d in range(1, X):
            stage3_recv(BACK, g, d)
        lax.fori_loop(g * HG, (g + 1) * HG, key_value_head, 0)

    def inputs_near():
        for d in (1, 3):
            core_send(d).start()

    def inputs_far():
        for d in (0, 1, 3):
            for way in range(2):
                y_pass_recv(lax.rem(x + d, X), way)
        y_far_recv(lax.rem(x + 2, X))
        core_send(2).start()

    def inputs_all():
        for d in range(Y):
            core_recv(d)

    queries(0)
    scans(MEM, 1)
    for g in range(G):
        line_sums(BACK, g)
    for way in range(2):
        y_recv(lax.rem(x + 2, X), way)
    inputs_near()

    def hops(j, way):
        odd = lax.rem(j, 2)
        return Z // 2 - 1 + odd if way == 0 else Z // 2 - odd

    def block(j, zt):
        return part[j, x_rows(lax.rem(zt + Z, Z))]

    def ring(j, way, s):
        zt = lax.rem(z + 1, Z) if way == 0 else lax.rem(z + Z - 1, Z)
        return rcopy(
            sb.at[j, way, s], rb.at[j, way, s], rs_s.at[j, way, s], rs_r.at[j, way, s], at_z(zt)
        )

    def target(j, way, s):
        left = hops(j, way) - s
        return z + left if way == 0 else z - left

    def weight_copy(j):
        return pltpu.make_async_copy(wout.at[j], weight_out.at[:, cols(j)], w_o.at[j])

    def product(j, carry):
        for way in range(2):
            qg_pass_recv(j, way)
        for i in range(2):
            r = pl.ds(i * (FEATURES // 2), FEATURES // 2)
            part[j, r] = dot(xt[r, :], qg[j], 1, 0)
        for way in range(2):
            sb[j, way, 0] = block(j, target(j, way, 0)).astype(BF16)
            ring(j, way, 0).start()
        return carry

    def level(s):
        def one(j, carry):
            for way in range(2):
                @pl.when(s < hops(j, way))
                def _():
                    ring(j, way, s - 1).wait_recv()
                    total = rb[j, way, s - 1].astype(F32) + block(j, target(j, way, s))
                    sb[j, way, s] = total.astype(BF16)
                    ring(j, way, s).start()

            return carry

        return one

    def finish(j, carry):
        total = block(j, z)
        for way in range(2):
            s = hops(j, way) - 1
            ring(j, way, s).wait_recv()
            total += rb[j, way, s].astype(F32)
        wout[j] = total
        weight_copy(j).start()
        return carry

    def slot(t, carry):
        @pl.when(t + LEAD < H)
        def _():
            for way in range(2):
                qg_send(t + LEAD, way).start()

        @pl.when(t < H)
        def _():
            for way in range(2):
                qg_recv(t, way)
                qg_pass(t, way).start()

        @pl.when(t == 0)
        def _():
            queries(1)

        @pl.when(t == 1)
        def _():
            inputs_far()

        @pl.when(t == LAG)
        def _():
            inputs_all()

        for s in range(Z // 2 + 1):
            j = t - LAG * (s + 1)
            step = product if s == 0 else finish if s == Z // 2 else level(s)

            @pl.when((j >= 0) & (j < H))
            def _():
                step(j, 0)

        @pl.when(t == H - LEAD)
        def _():
            for g in range(G):
                scans(BACK, g)

        for g in range(G):
            @pl.when(t == H + LAG * (g + 1))
            def _():
                keys_values(g)

        return carry

    lax.fori_loop(0, H + LAG * (1 + Z // 2), slot, 0)

    def drain(h, carry):
        for way in range(2):
            qg_send(h, way).wait_send()
            qg_pass(h, way).wait_send()
        for way in range(2):
            for s in range(Z // 2):
                @pl.when(s < hops(h, way))
                def _():
                    ring(h, way, s).wait_send()
        for c in kv_copies(h):
            c.wait()
        weight_copy(h).wait()
        return carry

    lax.fori_loop(0, H, drain, 0)
    for d in range(1, X):
        x_send(d).wait_send()
        for kind in range(2):
            for g in range(G):
                stage1(kind, g, d).wait_send()
                stage3(kind, g, d).wait_send()
    for xi in range(X):
        for way in range(2):
            y_send(xi, way).wait_send()
    for d in (0, 1, 3):
        for way in range(2):
            y_pass(lax.rem(x + d, X), way).wait_send()
    y_far(lax.rem(x + 2, X)).wait_send()
    for d in range(Y):
        core_send(d).wait_send()
    for g in range(G):
        def up(zt, carry):
            stage2(MEM, g, zt).wait_send()
            return carry

        def down(zt, carry):
            stage2(BACK, g, zt).wait_send()
            return carry

        lax.fori_loop(z + 1, Z, up, 0)
        lax.fori_loop(0, z, down, 0)


def widen_kernel(key_low, value_low, weight, key_out, value_out, weight_out):
    key_out[...] = key_low[...].astype(F32)
    value_out[...] = value_low[...].astype(F32)
    weight_out[...] = weight[...]


def widen(key_grad, value_grad, weight_grad):
    steps = 8
    tall = pl.BlockSpec((T // steps, H * W), lambda i: (i, 0))
    low = pl.BlockSpec((F // steps, H * W), lambda i: (i, 0))
    return pl.pallas_call(
        widen_kernel,
        grid=(steps,),
        out_shape=(
            jax.ShapeDtypeStruct((T, H * W), F32),
            jax.ShapeDtypeStruct((T, H * W), F32),
            jax.ShapeDtypeStruct((F, H * W), F32),
        ),
        in_specs=[tall, tall, low],
        out_specs=(tall, tall, low),
        compiler_params=pltpu.CompilerParams(vmem_limit_bytes=60 * 2**20),
    )(key_grad, value_grad, weight_grad)


def local(inputs, query, key_rows, value, grad_out, decay_power):
    dma = pltpu.SemaphoreType.DMA
    anywhere = pl.BlockSpec(memory_space=pl.ANY)
    key_grad, value_grad, weight_grad = pl.pallas_call(
        kernel,
        out_shape=(
            jax.ShapeDtypeStruct((T, H * W), BF16),
            jax.ShapeDtypeStruct((T, H * W), BF16),
            jax.ShapeDtypeStruct((F, H * W), F32),
        ),
        in_specs=[anywhere] * 5 + [pl.BlockSpec(memory_space=pltpu.SMEM)],
        out_specs=(anywhere,) * 3,
        scratch_shapes=[
            pltpu.VMEM((T, X * F), BF16),
            pltpu.VMEM((T, H * W), BF16),
            pltpu.VMEM((T, H * W), BF16),
            pltpu.VMEM((T, H * W), BF16),
            pltpu.VMEM((T, H * W), BF16),
            pltpu.VMEM((X * F, T), BF16),
            pltpu.VMEM((FEATURES, X * T), BF16),
            pltpu.VMEM((2, H, 8, W), F32),
            pltpu.VMEM((H, W, W), F32),
            pltpu.VMEM((H, W, W), F32),
            pltpu.VMEM((2, X, H, Q, W), BF16),
            pltpu.VMEM((2, X, H, Q, W), BF16),
            pltpu.VMEM((2, H, Q, W), BF16),
            pltpu.VMEM((Z, H, Q, W), BF16),
            pltpu.VMEM((2, X, H, Q, W), BF16),
            pltpu.VMEM((2, X, H, Q, W), BF16),
            pltpu.VMEM((H, T, W), F32),
            pltpu.VMEM((H, T, W), BF16),
            pltpu.VMEM((H, T, W), BF16),
            pltpu.VMEM((H, X * T, W), BF16),
            pltpu.VMEM((H, FEATURES, W), F32),
            pltpu.VMEM((H, 2, Z // 2, F, W), BF16),
            pltpu.VMEM((H, 2, Z // 2, F, W), BF16),
            pltpu.VMEM((H, F, W), F32),
            dma((5,)),
            dma,
            dma((X - 1,)),
            dma((X - 1,)),
            dma((X, 2)),
            dma((X, 2)),
            dma((X, 2)),
            dma((X, 2)),
            dma((Y,)),
            dma((Y,)),
            dma((2, G, X - 1)),
            dma((2, G, X - 1)),
            dma((G, Z)),
            dma((G, Z)),
            dma((2, G, X - 1)),
            dma((2, G, X - 1)),
            dma((H, 2)),
            dma((H, 2)),
            dma((H, 2)),
            dma((H, 2)),
            dma((H, 2, Z // 2)),
            dma((H, 2, Z // 2)),
            dma((2, H)),
            dma((H,)),
        ],
        compiler_params=pltpu.CompilerParams(
            collective_id=0, has_side_effects=True, vmem_limit_bytes=60 * 2**20
        ),
        cost_estimate=pl.CostEstimate(
            flops=9 * 10**9, bytes_accessed=10 * 2**20, transcendentals=10**6
        ),
    )(inputs, query, key_rows, value, grad_out, decay_power)
    return widen(key_grad, value_grad, weight_grad)


def solution(mesh):
    placed = (P("ctx", "head"),) * 5 + (P(),)
    return jax.shard_map(
        local,
        mesh=mesh,
        in_specs=placed,
        out_specs=(P("ctx", "head"),) * 3,
        check_vma=False,
    )
```
